32 devices in a mesh: dp: 4 (over y, core), expert: 8 (over z, x).
Axes of the slice: x: 2, y: 2, z: 4, core: 2. Of those that a mesh axis runs over, the one named last changes fastest.
Arguments:
- tokens: bfloat16 [384, 7168], P('expert'), may hold values from -6 to 6
- grad_out: bfloat16 [384, 7168], P('expert'), may hold values from -6 to 6
- routes: int32 [384, 2], P('expert'), may hold values from 0 to 7, all different within a row; in each aligned block of 48 rows (0 to 47, 48 to 95, ...) at most 15 rows name the same one
- gates: bfloat16 [384, 2], P('expert'), may hold values from 0.049804688 to 0.59765625
- w_gate: bfloat16 [8, 7168, 1024], P('expert', None, 'dp'), may hold values from -0.0625 to 0.0625
- w_up: bfloat16 [8, 7168, 1024], P('expert', None, 'dp'), may hold values from -0.0625 to 0.0625
- w_down: bfloat16 [8, 1024, 7168], P('expert', 'dp'), may hold values from -0.1875 to 0.1875
Outputs:
- grad_tokens: bfloat16 [384, 7168], P('expert', 'dp')
- grad_gates: float32 [384, 2], P('expert')
- grad_w_gate: bfloat16 [8, 7168, 1024], P('expert', None, 'dp')
- grad_w_up: bfloat16 [8, 7168, 1024], P('expert', None, 'dp')
- grad_w_down: bfloat16 [8, 1024, 7168], P('expert', 'dp')
The draws below stay inside these ranges and needn't reach their ends.
Inputs may be any that keep to these rules, and one draw needn't show every extreme that they name: `routes`: within each aligned block of 48 tokens no expert is named by more than 15 pairs, a bound that some block reaches; the 2 experts of one token differ.
All inputs are finite; a program needn't handle non-finite values.
Results may differ from the reference program's by a relative error of at most 0.02.
Values may be sent and summed in bfloat16 or wider, within the bound.
A program may use at most 128 MiB of HBM per device.

```python
import math
import jax
import jax.numpy as jnp
import numpy as np
from jax import lax

D = 7168
FFE = 1024
TOK_DEV = 48
EXPERTS = 8
TOPK = 2
CAP = 15
SLOTS = 120
HID_DEV = 256
TOKENS = 384
N_DP = 4
N_EXPERT = 8


def block_levels(stream_key, extent, split, smallest, top_value):
    level = 1.0
    for dim, shards_of in split:
        steps = jax.random.uniform(jax.random.fold_in(jax.random.fold_in(stream_key, 6), dim), (shards_of,), jnp.float32, smallest / len(split), top_value / len(split))
        level = level * jnp.repeat(jnp.exp(steps), extent[dim] // shards_of).reshape((-1,) + (1,) * (len(extent) - 1 - dim))
    return level


def assign_block(stream_key, own, number, rows, number_of, top, reach, slope):
    order = jax.random.permutation(stream_key, number_of)
    crowded, common = load_shares(number_of, rows * top, reach, slope, True), load_shares(number_of, rows * top, reach, slope, False)
    places = jnp.arange(number_of)

    def named(sizes, turn):
        used = int((sizes > 0).sum())
        fixed = max(1, used // 4)
        moved = fixed + (places - fixed + turn * (used - fixed)) % max(1, number_of - fixed)
        return jnp.zeros((number_of,), jnp.int32).at[order[jnp.where(places < fixed, places, moved)]].set(jnp.asarray(sizes, jnp.int32))

    sizes = jnp.where(number % 4 == 0, named(crowded, number // 4), named(common, number - number // 4 - 1))
    mixed = jax.random.permutation(jax.random.fold_in(own, 3), number_of)
    source_of, sink = mixed[0:number_of // 2 * 2:2], mixed[1:number_of // 2 * 2:2]
    slack = jnp.minimum(sizes[source_of] - 1, reach - sizes[sink]) // 2
    slack = jnp.where((source_of == order[0]) | (sink == order[0]) | (sizes[sink] == 0), 0, jnp.maximum(slack, 0))
    moved = jax.random.randint(jax.random.fold_in(own, 4), (number_of // 2,), 0, 1 << 20) % (slack + 1)
    sizes = sizes.at[source_of].add(-moved).at[sink].add(moved)
    members = jnp.searchsorted(jnp.cumsum(sizes), jnp.arange(rows * top), side="right").astype(jnp.int32)
    listing = members.reshape(top, rows).T
    listing = listing[jax.random.permutation(jax.random.fold_in(own, 1), rows)]
    turn = jax.random.randint(jax.random.fold_in(own, 2), (rows, 1), 0, top)
    return jnp.take_along_axis(listing, (jnp.arange(top)[None, :] + turn) % top, axis=1)


def load_shares(amount, total, limit, skew, full):
    loads = [(1 << 20) // math.isqrt(standing ** skew) + 1 for standing in range(1, amount + 1)]
    largest = limit if full else min(limit, max(-(-total // amount), total * loads[0] // sum(loads)))
    least = 1 if total - largest >= amount - 1 else 0
    given, surplus = [largest] + [least] * (amount - 1), total - largest - least * (amount - 1)
    while surplus > 0:
        candidates = [i for i in range(1, amount) if given[i] < largest] or [i for i in range(1, amount) if given[i] < limit]
        pool, left = sum([loads[i] for i in candidates]), surplus
        for i in candidates:
            more = min(limit - given[i], max(1, left * loads[i] // pool), surplus)
            given[i] = given[i] + more
            surplus = surplus - more
    return np.array(given)


def centred(key, shape, width, reach, pieces=(), held_as=jnp.bfloat16):
    gain = block_levels(key, shape, pieces, -0.22, 0.18) if pieces else 1.0
    drawn = jax.random.normal(key, shape, jnp.float32) * width * gain
    return jnp.minimum(jnp.maximum(drawn, -reach), reach).astype(held_as)


def setup_inputs(seed: int = 0) -> dict:
    arg_keys = jax.random.split(jax.random.key(seed), 8)
    tokens = centred(arg_keys[0], (TOKENS, D), 1.0, 6.0, ((0, 8),))
    grad_out = centred(arg_keys[1], (TOKENS, D), 1.0, 6.0, ((0, 8),))
    routes_keys = jax.random.split(jax.random.fold_in(arg_keys[2], 1), TOKENS // TOK_DEV)
    routes_turns = jax.random.permutation(jax.random.fold_in(arg_keys[2], 3), TOKENS // TOK_DEV)
    routes = jax.vmap(lambda own, number: assign_block(jax.random.fold_in(arg_keys[2], 2), own, number, TOK_DEV, EXPERTS, TOPK, CAP, 2))(routes_keys, routes_turns).reshape((TOKENS, TOPK))
    gates = jnp.clip(0.049804688 + 0.54785156 * jax.random.uniform(arg_keys[3], (TOKENS, TOPK), jnp.float32) ** block_levels(arg_keys[3], (TOKENS, TOPK), ((0, 8),), -0.2, 0.2), 0.049804688, 0.59765625).astype(jnp.bfloat16)
    w_gate = centred(arg_keys[4], (EXPERTS, D, FFE), D ** -0.5, 0.0625, ((0, 8), (2, 4)))
    w_up = centred(arg_keys[5], (EXPERTS, D, FFE), D ** -0.5, 0.0625, ((0, 8), (2, 4)))
    w_down = centred(arg_keys[6], (EXPERTS, FFE, D), FFE ** -0.5, 0.1875, ((0, 8), (1, 4)))
    return {"tokens": tokens, "grad_out": grad_out, "routes": routes, "gates": gates, "w_gate": w_gate, "w_up": w_up, "w_down": w_down}


def slots_of(routes):
    blocks = routes.reshape(N_EXPERT, TOK_DEV * TOPK)
    onehot = (blocks[:, :, None] == jnp.arange(EXPERTS, dtype=jnp.int32)[None, None, :]).astype(jnp.int32)
    earlier = jnp.cumsum(onehot, axis=1) - onehot
    position = jnp.sum(earlier * onehot, axis=2)
    source = jnp.arange(N_EXPERT, dtype=jnp.int32)[:, None]
    return (source * CAP + position).reshape(TOKENS, TOPK).astype(jnp.int32)


def one_expert(packed):
    expert_in, expert_grad, weight_in, gate_mat, up_mat, down_mat = packed
    pre_gate = jnp.dot(expert_in, gate_mat, preferred_element_type=jnp.float32)
    pre_up = jnp.dot(expert_in, up_mat, preferred_element_type=jnp.float32)
    sigmoid_gate = jax.nn.sigmoid(pre_gate)
    activated = pre_gate * sigmoid_gate
    hidden = activated * pre_up
    stored = hidden.astype(jnp.bfloat16)
    back = jnp.dot(expert_grad, down_mat.T, preferred_element_type=jnp.float32)
    gate_terms = jnp.sum(stored.astype(jnp.float32) * back, axis=1)
    weight_col = weight_in.astype(jnp.float32)[:, None]
    scaled = (weight_col * hidden).astype(jnp.bfloat16)
    grad_down = jnp.dot(scaled.T, expert_grad, preferred_element_type=jnp.float32).astype(jnp.bfloat16)
    weighted = weight_col * back
    d_up = (weighted * activated).astype(jnp.bfloat16)
    d_gate = (weighted * pre_up * sigmoid_gate * (1.0 + pre_gate * (1.0 - sigmoid_gate))).astype(jnp.bfloat16)
    grad_gate = jnp.dot(expert_in.T, d_gate, preferred_element_type=jnp.float32).astype(jnp.bfloat16)
    grad_up = jnp.dot(expert_in.T, d_up, preferred_element_type=jnp.float32).astype(jnp.bfloat16)
    gate_blocks = d_gate.reshape(SLOTS, N_DP, HID_DEV).astype(jnp.float32)
    up_blocks = d_up.reshape(SLOTS, N_DP, HID_DEV).astype(jnp.float32)
    gate_wblocks = gate_mat.reshape(D, N_DP, HID_DEV).astype(jnp.float32)
    up_wblocks = up_mat.reshape(D, N_DP, HID_DEV).astype(jnp.float32)
    parts = jnp.einsum("snh,dnh->nsd", gate_blocks, gate_wblocks) + jnp.einsum("snh,dnh->nsd", up_blocks, up_wblocks)
    block_sum = jnp.sum(parts.astype(jnp.bfloat16).astype(jnp.float32), axis=0)
    return grad_gate, grad_up, grad_down, gate_terms, block_sum


def reference(tokens, grad_out, routes, gates, w_gate, w_up, w_down):
    slot = slots_of(routes)
    flat_expert = routes.reshape(-1).astype(jnp.int32)
    flat_slot = slot.reshape(-1).astype(jnp.int32)
    token_index = jnp.repeat(jnp.arange(TOKENS, dtype=jnp.int32), TOPK)
    expert_in = jnp.zeros((EXPERTS, SLOTS, D), jnp.bfloat16).at[flat_expert, flat_slot].set(tokens[token_index])
    expert_grad = jnp.zeros((EXPERTS, SLOTS, D), jnp.bfloat16).at[flat_expert, flat_slot].set(grad_out[token_index])
    weight_in = jnp.zeros((EXPERTS, SLOTS), jnp.bfloat16).at[flat_expert, flat_slot].set(gates.reshape(-1))
    grad_gate, grad_up, grad_down, gate_terms, block_sum = lax.map(one_expert, (expert_in, expert_grad, weight_in, w_gate, w_up, w_down))
    picked = block_sum[routes, slot]
    grad_tokens = jnp.sum(picked, axis=1).astype(jnp.bfloat16)
    grad_gates = gate_terms[routes, slot]
    return grad_tokens, grad_gates, grad_gate, grad_up, grad_down
```

```python
import jax
import jax.numpy as jnp
from jax import lax
from jax.sharding import PartitionSpec as P

CONTRACT_LAST = (((1,), (1,)), ((), ()))
CONTRACT_FIRST = (((0,), (0,)), ((), ()))
LANES = 128
ROWS = 16


def on_device(tokens, grad_out, routes, gates, w_gate, w_up, w_down):
    experts = lax.axis_size("expert")
    groups = lax.axis_size("dp")
    part = lax.axis_index("dp")
    tok_rows, width_full = tokens.shape
    top = routes.shape[1]
    cap = tok_rows * top * 5 // (experts * 4)
    room = (cap + ROWS - 1) // ROWS * ROWS
    slots = experts * room
    width = width_full // groups
    flat = routes.reshape(-1)
    pair = jnp.arange(flat.shape[0], dtype=jnp.int32)
    earlier = (flat[:, None] == flat[None, :]) & (pair[None, :] < pair[:, None])
    position = jnp.sum(earlier.astype(jnp.int32), axis=1)
    slot_of = (flat * room + position).reshape(tok_rows, top)
    match = slot_of[None, :, :] == jnp.arange(slots, dtype=jnp.int32)[:, None, None]
    place = jnp.any(match, axis=2).astype(jnp.bfloat16)
    gate_slots = jnp.sum(jnp.where(match, gates.astype(jnp.float32)[None, :, :], 0.0), axis=(1, 2))
    gate_slots = gate_slots.astype(jnp.bfloat16)

    def fill(source):
        share = lax.dynamic_slice_in_dim(source, part * width, width, axis=1)
        return jnp.dot(place, share, preferred_element_type=jnp.float32).astype(jnp.bfloat16)

    def swap(sent):
        swapped = lax.all_to_all(
            sent.reshape(experts, room, sent.shape[1]), "expert", split_axis=0, concat_axis=0, tiled=True
        )
        return swapped.reshape(slots, sent.shape[1])

    def join(shares):
        whole = lax.all_gather(shares, "dp", axis=0)
        return whole.transpose(1, 0, 2).reshape(slots, width_full)

    expert_in = join(swap(fill(tokens)))
    weight_lanes = jnp.pad(gate_slots[:, None], ((0, 0), (0, LANES - 1)))
    recv_grad = swap(jnp.concatenate([fill(grad_out), weight_lanes], axis=1))
    expert_grad = join(recv_grad[:, :width])
    weight_col = recv_grad[:, width : width + 1].astype(jnp.float32)
    gate_mat = w_gate[0]
    up_mat = w_up[0]
    down_mat = w_down[0]
    pre_gate = jnp.dot(expert_in, gate_mat, preferred_element_type=jnp.float32)
    pre_up = jnp.dot(expert_in, up_mat, preferred_element_type=jnp.float32)
    sigmoid_gate = jax.nn.sigmoid(pre_gate)
    activated = pre_gate * sigmoid_gate
    hidden = activated * pre_up
    stored = hidden.astype(jnp.bfloat16)
    back = lax.dot_general(expert_grad, down_mat, CONTRACT_LAST, preferred_element_type=jnp.float32)
    gate_terms = jnp.sum(stored.astype(jnp.float32) * back, axis=1)
    scaled = (weight_col * hidden).astype(jnp.bfloat16)
    grad_down = lax.dot_general(
        scaled, expert_grad, CONTRACT_FIRST, preferred_element_type=jnp.float32
    ).astype(jnp.bfloat16)
    weighted = weight_col * back
    d_up = (weighted * activated).astype(jnp.bfloat16)
    d_gate = (weighted * pre_up * sigmoid_gate * (1.0 + pre_gate * (1.0 - sigmoid_gate))).astype(
        jnp.bfloat16
    )
    grad_gate = lax.dot_general(
        expert_in, d_gate, CONTRACT_FIRST, preferred_element_type=jnp.float32
    ).astype(jnp.bfloat16)
    grad_up = lax.dot_general(
        expert_in, d_up, CONTRACT_FIRST, preferred_element_type=jnp.float32
    ).astype(jnp.bfloat16)
    high = gate_terms.astype(jnp.bfloat16)
    low = (gate_terms - high.astype(jnp.float32)).astype(jnp.bfloat16)
    term_lanes = jnp.pad(jnp.stack([high, low], axis=1), ((0, 0), (0, LANES - 2)))

    def block(n):
        rows = slice(n * width, (n + 1) * width)
        first = lax.dot_general(d_gate, gate_mat[rows], CONTRACT_LAST, preferred_element_type=jnp.float32)
        second = lax.dot_general(d_up, up_mat[rows], CONTRACT_LAST, preferred_element_type=jnp.float32)
        return jnp.concatenate([(first + second).astype(jnp.bfloat16), term_lanes], axis=1)

    blocks = jnp.concatenate([block(n) for n in range(groups)], axis=0)
    summed = lax.psum_scatter(blocks, "dp", scatter_dimension=0, tiled=True)
    back_home = swap(summed)
    token_grad = lax.dot_general(
        place, back_home[:, :width], CONTRACT_FIRST, preferred_element_type=jnp.float32
    )
    gate_flat = jnp.sum(back_home[:, width : width + 2].astype(jnp.float32), axis=1)
    grad_gates = jnp.sum(jnp.where(match, gate_flat[:, None, None], 0.0), axis=0)
    return (
        token_grad.astype(jnp.bfloat16),
        grad_gates,
        grad_gate[None],
        grad_up[None],
        grad_down[None],
    )


def solution(mesh):
    placed = (
        P("expert", None),
        P("expert", None),
        P("expert", None),
        P("expert", None),
        P("expert", None, "dp"),
        P("expert", None, "dp"),
        P("expert", "dp", None),
    )
    return jax.shard_map(
        on_device,
        mesh=mesh,
        in_specs=placed,
        out_specs=(
            P("expert", "dp"),
            P("expert", None),
            P("expert", None, "dp"),
            P("expert", None, "dp"),
            P("expert", "dp", None),
        ),
        check_vma=False,
    )
```

```python
import jax
import jax.numpy as jnp
from jax import lax
from jax.sharding import PartitionSpec as P

CONTRACT_LAST = (((1,), (1,)), ((), ()))
CONTRACT_FIRST = (((0,), (0,)), ((), ()))
LANES = 128
ROWS = 16


def on_device(tokens, grad_out, routes, gates, w_gate, w_up, w_down):
    experts = lax.axis_size("expert")
    groups = lax.axis_size("dp")
    part = lax.axis_index("dp")
    tok_rows, width_full = tokens.shape
    top = routes.shape[1]
    cap = tok_rows * top * 5 // (experts * 4)
    room = (cap + ROWS - 1) // ROWS * ROWS
    slots = experts * room
    width = width_full // groups
    flat = routes.reshape(-1)
    pair = jnp.arange(flat.shape[0], dtype=jnp.int32)
    earlier = (flat[:, None] == flat[None, :]) & (pair[None, :] < pair[:, None])
    position = jnp.sum(earlier.astype(jnp.int32), axis=1)
    slot_of = (flat * room + position).reshape(tok_rows, top)
    match = slot_of[None, :, :] == jnp.arange(slots, dtype=jnp.int32)[:, None, None]
    place = jnp.any(match, axis=2).astype(jnp.bfloat16)
    gate_slots = jnp.sum(jnp.where(match, gates.astype(jnp.float32)[None, :, :], 0.0), axis=(1, 2))
    gate_slots = gate_slots.astype(jnp.bfloat16)

    def fill(source):
        share = lax.dynamic_slice_in_dim(source, part * width, width, axis=1)
        return jnp.dot(place, share, preferred_element_type=jnp.float32).astype(jnp.bfloat16)

    def swap(sent):
        swapped = lax.all_to_all(
            sent.reshape(experts, room, sent.shape[1]), "expert", split_axis=0, concat_axis=0, tiled=True
        )
        return swapped.reshape(slots, sent.shape[1])

    def join(shares):
        whole = lax.all_gather(shares, "dp", axis=0)
        return whole.transpose(1, 0, 2).reshape(slots, width_full)

    def hop(sent, distance):
        return lax.ppermute(sent, "dp", [(i, i ^ distance) for i in range(groups)])

    def join_direct(share, far):
        whole = jnp.zeros((groups, slots, width), share.dtype)
        for k, chunk in enumerate([share] + far):
            whole = lax.dynamic_update_index_in_dim(whole, chunk, part ^ (2 * k), 0)
            whole = lax.dynamic_update_index_in_dim(whole, hop(chunk, 1), part ^ (2 * k + 1), 0)
        return whole.transpose(1, 0, 2).reshape(slots, width_full)

    expert_in = join(swap(fill(tokens)))
    weight_lanes = jnp.pad(gate_slots[:, None], ((0, 0), (0, LANES - 1)))
    recv_grad = swap(jnp.concatenate([fill(grad_out), weight_lanes], axis=1))
    grad_share = recv_grad[:, :width]
    grad_far = [hop(grad_share, 2 * k) for k in range(1, groups // 2)]
    weight_col = recv_grad[:, width : width + 1].astype(jnp.float32)
    gate_mat = w_gate[0]
    up_mat = w_up[0]
    down_mat = w_down[0]
    pre_gate = jnp.dot(expert_in, gate_mat, preferred_element_type=jnp.float32)
    pre_up = jnp.dot(expert_in, up_mat, preferred_element_type=jnp.float32)
    pre_gate, pre_up, grad_far = lax.optimization_barrier((pre_gate, pre_up, grad_far))
    expert_grad = join_direct(grad_share, grad_far)
    sigmoid_gate = jax.nn.sigmoid(pre_gate)
    activated = pre_gate * sigmoid_gate
    hidden = activated * pre_up
    stored = hidden.astype(jnp.bfloat16)
    back = lax.dot_general(expert_grad, down_mat, CONTRACT_LAST, preferred_element_type=jnp.float32)
    gate_terms = jnp.sum(stored.astype(jnp.float32) * back, axis=1)
    scaled = (weight_col * hidden).astype(jnp.bfloat16)
    grad_down = lax.dot_general(
        scaled, expert_grad, CONTRACT_FIRST, preferred_element_type=jnp.float32
    ).astype(jnp.bfloat16)
    weighted = weight_col * back
    d_up = (weighted * activated).astype(jnp.bfloat16)
    d_gate = (weighted * pre_up * sigmoid_gate * (1.0 + pre_gate * (1.0 - sigmoid_gate))).astype(
        jnp.bfloat16
    )
    grad_gate = lax.dot_general(
        expert_in, d_gate, CONTRACT_FIRST, preferred_element_type=jnp.float32
    ).astype(jnp.bfloat16)
    grad_up = lax.dot_general(
        expert_in, d_up, CONTRACT_FIRST, preferred_element_type=jnp.float32
    ).astype(jnp.bfloat16)
    high = gate_terms.astype(jnp.bfloat16)
    low = (gate_terms - high.astype(jnp.float32)).astype(jnp.bfloat16)
    term_lanes = jnp.pad(jnp.stack([high, low], axis=1), ((0, 0), (0, LANES - 2)))

    def block(owner):
        first = lax.dot_general(
            d_gate,
            lax.dynamic_slice_in_dim(gate_mat, owner * width, width, axis=0),
            CONTRACT_LAST,
            preferred_element_type=jnp.float32,
        )
        second = lax.dot_general(
            d_up,
            lax.dynamic_slice_in_dim(up_mat, owner * width, width, axis=0),
            CONTRACT_LAST,
            preferred_element_type=jnp.float32,
        )
        return jnp.concatenate([(first + second).astype(jnp.bfloat16), term_lanes], axis=1)

    def pair_sum(k):
        arrived = hop(block(part ^ (2 * k + 1)), 1)
        return arrived.astype(jnp.float32) + block(part ^ (2 * k)).astype(jnp.float32)

    arrivals = [hop(pair_sum(k).astype(jnp.bfloat16), 2 * k) for k in range(1, groups // 2)]
    total = pair_sum(0)
    for arrived in arrivals:
        total = total + arrived.astype(jnp.float32)
    summed = total.astype(jnp.bfloat16)
    back_home = swap(summed)
    token_grad = lax.dot_general(
        place, back_home[:, :width], CONTRACT_FIRST, preferred_element_type=jnp.float32
    )
    gate_flat = jnp.sum(back_home[:, width : width + 2].astype(jnp.float32), axis=1)
    grad_gates = jnp.sum(jnp.where(match, gate_flat[:, None, None], 0.0), axis=0)
    return (
        token_grad.astype(jnp.bfloat16),
        grad_gates,
        grad_gate[None],
        grad_up[None],
        grad_down[None],
    )


def solution(mesh):
    placed = (
        P("expert", None),
        P("expert", None),
        P("expert", None),
        P("expert", None),
        P("expert", None, "dp"),
        P("expert", None, "dp"),
        P("expert", "dp", None),
    )
    return jax.shard_map(
        on_device,
        mesh=mesh,
        in_specs=placed,
        out_specs=(
            P("expert", "dp"),
            P("expert", None),
            P("expert", None, "dp"),
            P("expert", None, "dp"),
            P("expert", "dp", None),
        ),
        check_vma=False,
    )
```

```python
import jax
import jax.numpy as jnp
from jax import lax
from jax.sharding import PartitionSpec as P

CONTRACT_LAST = (((1,), (1,)), ((), ()))
CONTRACT_FIRST = (((0,), (0,)), ((), ()))
LANES = 128
ROWS = 16


def on_device(tokens, grad_out, routes, gates, w_gate, w_up, w_down):
    experts = lax.axis_size("expert")
    groups = lax.axis_size("dp")
    part = lax.axis_index("dp")
    tok_rows, width_full = tokens.shape
    top = routes.shape[1]
    cap = tok_rows * top * 5 // (experts * 4)
    room = (cap + ROWS - 1) // ROWS * ROWS
    slots = experts * room
    width = width_full // groups
    flat = routes.reshape(-1)
    pair = jnp.arange(flat.shape[0], dtype=jnp.int32)
    earlier = (flat[:, None] == flat[None, :]) & (pair[None, :] < pair[:, None])
    position = jnp.sum(earlier.astype(jnp.int32), axis=1)
    slot_of = (flat * room + position).reshape(tok_rows, top)
    match = slot_of[None, :, :] == jnp.arange(slots, dtype=jnp.int32)[:, None, None]
    place = jnp.any(match, axis=2).astype(jnp.bfloat16)
    gate_slots = jnp.sum(jnp.where(match, gates.astype(jnp.float32)[None, :, :], 0.0), axis=(1, 2))
    gate_slots = gate_slots.astype(jnp.bfloat16)

    def fill(source):
        share = lax.dynamic_slice_in_dim(source, part * width, width, axis=1)
        return jnp.dot(place, share, preferred_element_type=jnp.float32).astype(jnp.bfloat16)

    def swap(sent):
        swapped = lax.all_to_all(
            sent.reshape(experts, room, sent.shape[1]), "expert", split_axis=0, concat_axis=0, tiled=True
        )
        return swapped.reshape(slots, sent.shape[1])

    def join(shares):
        whole = lax.all_gather(shares, "dp", axis=0)
        return whole.transpose(1, 0, 2).reshape(slots, width_full)

    def hop(sent, distance):
        return lax.ppermute(sent, "dp", [(i, i ^ distance) for i in range(groups)])

    def join_direct(share, far):
        chunks = []
        for chunk in [share] + far:
            chunks += [chunk, hop(chunk, 1)]
        ordered = []
        for n in range(groups):
            picked = chunks[0]
            for k in range(1, groups):
                picked = jnp.where(part == n ^ k, chunks[k], picked)
            ordered.append(picked)
        return jnp.concatenate(ordered, axis=1)

    expert_in = join(swap(fill(tokens)))
    weight_lanes = jnp.pad(gate_slots[:, None], ((0, 0), (0, LANES - 1)))
    recv_grad = swap(jnp.concatenate([fill(grad_out), weight_lanes], axis=1))
    grad_share = recv_grad[:, :width]
    grad_far = [hop(grad_share, 2 * k) for k in range(1, groups // 2)]
    weight_col = recv_grad[:, width : width + 1].astype(jnp.float32)
    gate_mat = w_gate[0]
    up_mat = w_up[0]
    down_mat = w_down[0]
    pre_gate = jnp.dot(expert_in, gate_mat, preferred_element_type=jnp.float32)
    pre_up = jnp.dot(expert_in, up_mat, preferred_element_type=jnp.float32)
    pre_gate, pre_up, grad_far = lax.optimization_barrier((pre_gate, pre_up, grad_far))
    expert_grad = join_direct(grad_share, grad_far)
    sigmoid_gate = jax.nn.sigmoid(pre_gate)
    activated = pre_gate * sigmoid_gate
    hidden = activated * pre_up
    stored = hidden.astype(jnp.bfloat16)
    back = lax.dot_general(expert_grad, down_mat, CONTRACT_LAST, preferred_element_type=jnp.float32)
    gate_terms = jnp.sum(stored.astype(jnp.float32) * back, axis=1)
    scaled = (weight_col * hidden).astype(jnp.bfloat16)
    grad_down = lax.dot_general(
        scaled, expert_grad, CONTRACT_FIRST, preferred_element_type=jnp.float32
    ).astype(jnp.bfloat16)
    weighted = weight_col * back
    d_up = (weighted * activated).astype(jnp.bfloat16)
    d_gate = (weighted * pre_up * sigmoid_gate * (1.0 + pre_gate * (1.0 - sigmoid_gate))).astype(
        jnp.bfloat16
    )
    grad_gate = lax.dot_general(
        expert_in, d_gate, CONTRACT_FIRST, preferred_element_type=jnp.float32
    ).astype(jnp.bfloat16)
    grad_up = lax.dot_general(
        expert_in, d_up, CONTRACT_FIRST, preferred_element_type=jnp.float32
    ).astype(jnp.bfloat16)
    high = gate_terms.astype(jnp.bfloat16)
    low = (gate_terms - high.astype(jnp.float32)).astype(jnp.bfloat16)
    term_lanes = jnp.pad(jnp.stack([high, low], axis=1), ((0, 0), (0, LANES - 2)))

    def block(owner, gate_side):
        first = lax.dot_general(
            gate_side,
            lax.dynamic_slice_in_dim(gate_mat, owner * width, width, axis=0),
            CONTRACT_LAST,
            preferred_element_type=jnp.float32,
        )
        second = lax.dot_general(
            d_up,
            lax.dynamic_slice_in_dim(up_mat, owner * width, width, axis=0),
            CONTRACT_LAST,
            preferred_element_type=jnp.float32,
        )
        return jnp.concatenate([(first + second).astype(jnp.bfloat16), term_lanes], axis=1)

    gate_side = d_gate
    arrivals = []
    for k in list(range(1, groups // 2)) + [0]:
        leaving = block(part ^ (2 * k + 1), gate_side)
        leaving, gate_side = lax.optimization_barrier((leaving, gate_side))
        arrived = hop(leaving, 1)
        kept = block(part ^ (2 * k), gate_side)
        pair = arrived.astype(jnp.float32) + kept.astype(jnp.float32)
        if k:
            pair, gate_side = lax.optimization_barrier((pair.astype(jnp.bfloat16), gate_side))
            arrivals.append(hop(pair, 2 * k))
        else:
            total = pair
    for arrived in arrivals:
        total = total + arrived.astype(jnp.float32)
    summed = total.astype(jnp.bfloat16)
    back_home = swap(summed)
    token_grad = lax.dot_general(
        place, back_home[:, :width], CONTRACT_FIRST, preferred_element_type=jnp.float32
    )
    gate_flat = jnp.sum(back_home[:, width : width + 2].astype(jnp.float32), axis=1)
    grad_gates = jnp.sum(jnp.where(match, gate_flat[:, None, None], 0.0), axis=0)
    return (
        token_grad.astype(jnp.bfloat16),
        grad_gates,
        grad_gate[None],
        grad_up[None],
        grad_down[None],
    )


def solution(mesh):
    placed = (
        P("expert", None),
        P("expert", None),
        P("expert", None),
        P("expert", None),
        P("expert", None, "dp"),
        P("expert", None, "dp"),
        P("expert", "dp", None),
    )
    return jax.shard_map(
        on_device,
        mesh=mesh,
        in_specs=placed,
        out_specs=(
            P("expert", "dp"),
            P("expert", None),
            P("expert", None, "dp"),
            P("expert", None, "dp"),
            P("expert", "dp", None),
        ),
        check_vma=False,
    )
```
